256 devices in a mesh: seq: 16 (over z, core), tensor: 16 (over y, x).
Axes of the slice: x: 4, y: 4, z: 8, core: 2. Of those that a mesh axis runs over, the one named last changes fastest.
Arguments:
- hidden_states: bfloat16 [24576, 8192], P('seq', 'tensor'), may hold values from -600 to 600, as said below
- gate_values: bfloat16 [24576, 8192], P('seq', 'tensor'), may hold values from -6 to 6
- norm_weight: float32 [8192], P('tensor'), may hold values from 0.1 to 1.9
- out_weight: bfloat16 [4096, 8192], P(None, 'tensor'), may hold values from -0.09375 to 0.09375
- out_grad: bfloat16 [24576, 4096], P('seq', 'tensor'), may hold values from -6 to 6
Outputs:
- grad_hidden: bfloat16 [24576, 8192], P('seq', 'tensor')
- grad_gate: bfloat16 [24576, 8192], P('seq', 'tensor')
- grad_out_weight: float32 [4096, 8192], P('seq', 'tensor')
- grad_norm_weight: float32 [8192], P('tensor')
The draws below stay inside these ranges and needn't reach their ends.
Inputs may be any that keep to these rules, and one draw needn't show every extreme that they name: `hidden_states`: finite values of the state-space scan's output.
All inputs are finite; a program needn't handle non-finite values.
Results may differ from the reference program's by a relative error of at most 0.0031.
Values may be sent and summed in bfloat16 or wider, within the bound.
No kernel may reach another device: no remote copies, remote signals or barrier semaphores. Data moves between devices by JAX's collectives and lax.ppermute only.
A program may use at most 128 MiB of HBM per device.

```python
import math
import jax
import jax.numpy as jnp
from jax import lax

D = 4096
DI = 8192
TOK_DEV = 1536
GROUP = 8192
TOKENS = 24576


def draw_hidden_states(key, part):
    key = jax.random.fold_in(key, 17)
    key_values, key_columns, key_scales = jax.random.split(key, 3)
    channel = jnp.arange(DI, dtype=jnp.float32)
    columns = jnp.exp(math.log(3.0) * channel / DI + jax.random.uniform(key_columns, (DI,), jnp.float32, 0.0, math.log(4.0)))
    row_top = math.log(10.0)
    values_raw = jax.random.truncated_normal(key_values, -5.0, 5.0, (TOKENS, DI), jnp.float32)
    scales = jnp.exp(jax.random.uniform(key_scales, (TOKENS, 1), jnp.float32, 0.0, row_top))
    return (values_raw * scales * columns[None, :]).astype(jnp.bfloat16)


def with_spikes(entries, rng, source, target, shards_of, factor):
    owner, partner = [(jnp.arange(entries.shape[dim]) // (entries.shape[dim] // shards_of)).reshape([-1 if axis == dim else 1 for axis in range(entries.ndim)]) for dim in (source, target)]
    chosen = jax.random.permutation(rng, shards_of)[partner]
    strong = (owner == chosen) | (owner == (partner + shards_of // 2) % shards_of)
    return jnp.where(strong, factor * entries, entries)


def block_levels(stream_key, dims, shards, smallest, largest):
    level, own = 1.0, jax.random.fold_in(stream_key, 6)
    for dim, shards_of in shards:
        draws = jnp.exp(jax.random.uniform(jax.random.fold_in(own, dim), (shards_of,), jnp.float32, smallest / len(shards), largest / len(shards)))
        level = level * jnp.repeat(draws, dims[dim] // shards_of).reshape([-1 if axis == dim else 1 for axis in range(len(dims))])
    return level


def noise(stream_key, shape, width, bound, cuts=(), kind=jnp.bfloat16):
    values = width * jax.random.normal(stream_key, shape, jnp.float32)
    if cuts:
        values = values * block_levels(stream_key, shape, cuts, -0.22, 0.18)
    return jnp.clip(values, -bound, bound).astype(kind)


def bell_draw_with(stream_key, extent, spread, limit, cuts, heavy, held_as=jnp.bfloat16):
    entries = spread * jax.random.normal(stream_key, extent, jnp.float32)
    if cuts:
        entries = entries * block_levels(stream_key, extent, cuts, -0.22, 0.18)
    return jnp.clip(with_spikes(entries, jax.random.fold_in(stream_key, 3), *heavy), -limit, limit).astype(held_as)


def setup_inputs(seed: int = 0) -> dict:
    key_of = jax.random.split(jax.random.key(seed), 6)
    return {
        "hidden_states": draw_hidden_states(jax.random.fold_in(key_of[5], 71), 0),
        "gate_values": noise(key_of[1], (TOKENS, DI), 1.0, 6.0, ((0, 16), (1, 16))),
        "norm_weight": jnp.clip(1.0 + 0.18 * jax.random.normal(key_of[2], (DI,), jnp.float32), 0.1, 1.9),
        "out_weight": noise(key_of[3], (D, DI), D ** -0.5, 0.09375, ((1, 16),)),
        "out_grad": bell_draw_with(key_of[4], (TOKENS, D), 1.0, 6.0, ((0, 16), (1, 16)), (0, 1, 16, 2.0)),
    }


def reference(hidden_states, gate_values, norm_weight, out_weight, out_grad):
    group_count = DI // GROUP
    block_count = TOKENS // TOK_DEV
    hidden_blocks = hidden_states.reshape(block_count, TOK_DEV, DI)
    gate_blocks = gate_values.reshape(block_count, TOK_DEV, DI)
    grad_blocks = out_grad.reshape(block_count, TOK_DEV, D)

    def one_block(carry, inputs):
        weight_acc, gain_acc = carry
        hidden_part, gate_part, grad_part = inputs
        gate_wide = gate_part.astype(jnp.float32)
        sigmoid_gate = jax.nn.sigmoid(gate_wide)
        gate_silu = gate_wide * sigmoid_gate
        hidden_wide = hidden_part.astype(jnp.float32)
        gated = (hidden_wide * gate_silu).reshape(TOK_DEV, group_count, GROUP)
        mean_square = lax.optimization_barrier(jnp.sum(gated * gated, axis=-1, keepdims=True)) / GROUP
        inverse_rms = 1.0 / jnp.sqrt(mean_square + 1e-05)
        normalized = (gated * inverse_rms).reshape(TOK_DEV, DI)
        normed = (normalized * norm_weight).astype(jnp.bfloat16)
        grad_normed = jnp.dot(grad_part, out_weight, preferred_element_type=jnp.float32)
        weighted = (grad_normed * norm_weight).reshape(TOK_DEV, group_count, GROUP)
        group_product = lax.optimization_barrier(jnp.sum(weighted * gated, axis=-1, keepdims=True)) / GROUP
        grad_gated = (inverse_rms * (weighted - gated * inverse_rms * inverse_rms * group_product)).reshape(TOK_DEV, DI)
        grad_hidden = (grad_gated * gate_silu).astype(jnp.bfloat16)
        grad_gate = (grad_gated * hidden_wide * sigmoid_gate * (1.0 + gate_wide * (1.0 - sigmoid_gate))).astype(jnp.bfloat16)
        weight_acc = weight_acc + jnp.dot(grad_part.T, normed, preferred_element_type=jnp.float32)
        gain_acc = gain_acc + lax.optimization_barrier(jnp.sum(grad_normed * normalized, axis=0))
        return ((weight_acc, gain_acc), (grad_hidden, grad_gate))
    start = (jnp.zeros((D, DI), jnp.float32), jnp.zeros((DI,), jnp.float32))
    (weight_acc, gain_acc), (grad_hidden, grad_gate) = lax.scan(one_block, start, (hidden_blocks, gate_blocks, grad_blocks))
    return (grad_hidden.reshape(TOKENS, DI), grad_gate.reshape(TOKENS, DI), weight_acc, gain_acc)
```

```python
import jax
import jax.numpy as jnp
from jax import lax
from jax.experimental import pallas as pl
from jax.experimental.pallas import tpu as pltpu
from jax.sharding import PartitionSpec as P

DI = 8192
BF = jnp.bfloat16
F32 = jnp.float32
AXES = ("seq", "tensor")
SY = SX = 4
SZ = 8
FEAT = 128


def pairs(move):
    table = []
    for z in range(SZ):
        for c in range(2):
            for y in range(SY):
                for x in range(SX):
                    z2, c2, y2, x2 = move(z, c, y, x)
                    target = ((z2 % SZ) * 2 + c2) * 16 + (y2 % SY) * 4 + x2 % SX
                    table.append(((z * 2 + c) * 16 + y * 4 + x, target))
    return table


def first(d):
    return pairs(lambda z, c, y, x: (z, c, y + (d if c else 0), x + (0 if c else d)))


def second(d):
    return pairs(lambda z, c, y, x: (z, c, y + (0 if c else d), x + (d if c else 0)))


def along_z(d):
    return pairs(lambda z, c, y, x: (z + d, c, y, x))


def send(value, table):
    return lax.ppermute(value, AXES, table)


SWAP = pairs(lambda z, c, y, x: (z, 1 - c, y, x))


def block_ids(core, y0, x0):
    ids = []
    for j, members in ((0, (0, -1, 1, 2)), (-1, (0, -1, 1, 2)), (1, (0, -1, 1, 2)), (2, (0, -1, 1, 2))):
        for i in members:
            a = (y0 + j) % 4 * 4 + (x0 + i) % 4
            b = (y0 + i) % 4 * 4 + (x0 + j) % 4
            ids.append(jnp.where(core == 0, a, b))
    return ids


def chunk_body(has_acc, chunk, *refs):
    if has_acc:
        ids, s, r, l, rf, lf, w, normed, acc_in, gn, mine, other, xs, ws, go, sx, sw, so, sa = refs
    else:
        ids, s, r, l, rf, lf, w, normed, gn, mine, other, xs, ws, go, sx, sw, so = refs
    sources = [(s, i) for i in range(4)] + [(r, i) for i in range(4)] + [(l, i) for i in range(4)]
    sources += [(rf, 0), (rf, 1), (lf, 0), (lf, 1)]
    copies = []
    for n, (ref, i) in enumerate(sources):
        g, k = n // 4, n % 4
        cx = pltpu.make_async_copy(ref.at[i], xs.at[g, :, pl.ds(k * FEAT, FEAT)], sx.at[n])
        row = pl.multiple_of(ids[n] * (2 * FEAT) + chunk * FEAT, FEAT)
        cw = pltpu.make_async_copy(w.at[pl.ds(row, FEAT), :], ws.at[g, pl.ds(k * FEAT, FEAT), :], sw.at[n])
        cx.start()
        cw.start()
        copies.append((cx, cw))
    if has_acc:
        ca = pltpu.make_async_copy(acc_in, gn, sa)
        ca.start()
    for g in range(4):
        for k in range(4):
            copies[4 * g + k][0].wait()
            copies[4 * g + k][1].wait()
        if g == 0 and has_acc:
            ca.wait()
        tile = 256

        @pl.loop(0, 1536 // tile)
        def _(t):
            rows = pl.ds(pl.multiple_of(t * tile, tile), tile)
            part = jnp.dot(xs[g, rows, :], ws[g], preferred_element_type=F32)
            if g == 0 and not has_acc:
                gn[rows, :] = part
            else:
                gn[rows, :] += part

        for k in range(4):
            n = 4 * g + k
            go[n] = lax.dot_general(
                xs[g, :, k * FEAT : (k + 1) * FEAT], normed[...], (((0,), (0,)), ((), ())),
                preferred_element_type=F32,
            )
            place = ids[16 + n]

            @pl.when(place < SZ)
            def _():
                pltpu.make_async_copy(go.at[n], mine.at[place], so.at[n]).start()

            @pl.when(place >= SZ)
            def _():
                pltpu.make_async_copy(go.at[n], other.at[place - SZ], so.at[n]).start()

    for n in range(16):
        pltpu.make_async_copy(go.at[n], mine.at[0], so.at[n]).wait()


def chunk_kernel(chunk, ids, parts, w, normed, acc):
    tok, ch = normed.shape
    has_acc = acc is not None
    anyspace = pl.BlockSpec(memory_space=pl.ANY)
    whole = pl.BlockSpec(memory_space=pltpu.VMEM)
    in_specs = [pl.BlockSpec(memory_space=pltpu.SMEM)] + [anyspace] * 6 + [whole]
    args = [ids, *parts, w, normed]
    scratch = [
        pltpu.VMEM((4, tok, 4 * FEAT), BF),
        pltpu.VMEM((4, 4 * FEAT, ch), BF),
        pltpu.VMEM((16, FEAT, ch), F32),
        pltpu.SemaphoreType.DMA((16,)),
        pltpu.SemaphoreType.DMA((16,)),
        pltpu.SemaphoreType.DMA((16,)),
    ]
    if has_acc:
        in_specs.append(anyspace)
        args.append(acc)
        scratch.append(pltpu.SemaphoreType.DMA(()))
    return pl.pallas_call(
        lambda *refs: chunk_body(has_acc, chunk, *refs),
        out_shape=(
            jax.ShapeDtypeStruct((tok, ch), F32),
            jax.ShapeDtypeStruct((SZ, FEAT, ch), F32),
            jax.ShapeDtypeStruct((SZ, FEAT, ch), F32),
        ),
        in_specs=in_specs,
        out_specs=(whole, anyspace, anyspace),
        scratch_shapes=scratch,
        compiler_params=pltpu.CompilerParams(vmem_limit_bytes=40 * 1024 * 1024),
        cost_estimate=pl.CostEstimate(flops=6_500_000_000, bytes_accessed=20_000_000, transcendentals=0),
        name="chunk%d" % chunk,
    )(*args)


def gather(value):
    near = [value, send(value, first(1)), send(value, first(-1)), send(value, first(2))]
    stack = jnp.stack(near)
    right = send(stack, second(1))
    left = send(stack, second(-1))
    return stack, right, left, send(right[:2], second(1)), send(left[2:], second(-1))


def total(value, axis):
    spread = jnp.broadcast_to(value[None], (16,) + value.shape)
    return jnp.sum(lax.all_to_all(spread, axis, 0, 0), axis=0)


def scatter_rows(mine, other):
    came = send(other, SWAP)
    own = mine[0] + came[0]
    result = own
    for k in (4, 3, -3, 2, -2, 1, -1):
        block = (mine[k % SZ] + came[k % SZ]).astype(BF)
        result = result + send(block, along_z(k)).astype(F32)
    return result


def local(hidden_states, gate_values, norm_weight, out_weight, out_grad):
    seq = lax.axis_index("seq")
    place = lax.axis_index("tensor")
    core, z0 = seq % 2, seq // 2
    blocks = block_ids(core, place // 4, place % 4)
    slots = [jnp.where(b % 2 == core, 0, SZ) + (b // 2 - z0) % SZ for b in blocks]
    ids = jnp.stack(blocks + slots).astype(jnp.int32)

    parts1 = gather(out_grad[:, :FEAT])
    parts2 = gather(out_grad[:, FEAT:])

    gate_wide = gate_values.astype(F32)
    sigmoid_gate = jax.nn.sigmoid(gate_wide)
    gate_silu = gate_wide * sigmoid_gate
    hidden_wide = hidden_states.astype(F32)
    gated = hidden_wide * gate_silu
    squares = total(jnp.sum(gated * gated, axis=-1), "tensor")
    inverse_rms = (1.0 / jnp.sqrt(squares / DI + 1e-05))[:, None]
    normalized = gated * inverse_rms
    normed = (normalized * norm_weight).astype(BF)

    grad1, mine1, other1 = chunk_kernel(0, ids, parts1, out_weight, normed, None)
    rows1 = scatter_rows(mine1, other1)
    grad_normed, mine2, other2 = chunk_kernel(1, ids, parts2, out_weight, normed, grad1)
    rows2 = scatter_rows(mine2, other2)

    weighted = grad_normed * norm_weight
    products = total(jnp.sum(weighted * gated, axis=-1), "tensor")
    group_product = (products / DI)[:, None]
    grad_norm_weight = total(jnp.sum(grad_normed * normalized, axis=0), "seq")
    grad_gated = inverse_rms * (weighted - gated * inverse_rms * inverse_rms * group_product)
    grad_hidden = (grad_gated * gate_silu).astype(BF)
    grad_gate = (
        grad_gated * hidden_wide * sigmoid_gate * (1.0 + gate_wide * (1.0 - sigmoid_gate))
    ).astype(BF)
    return grad_hidden, grad_gate, jnp.concatenate([rows1, rows2]), grad_norm_weight


def solution(mesh):
    return jax.shard_map(
        local,
        mesh=mesh,
        in_specs=(
            P("seq", "tensor"),
            P("seq", "tensor"),
            P("tensor"),
            P(None, "tensor"),
            P("seq", "tensor"),
        ),
        out_specs=(P("seq", "tensor"), P("seq", "tensor"), P("seq", "tensor"), P("tensor")),
        check_vma=False,
    )
```

```python
import jax
import jax.numpy as jnp
from jax import lax
from jax.experimental import pallas as pl
from jax.experimental.pallas import tpu as pltpu
from jax.sharding import PartitionSpec as P

DI = 8192
BF = jnp.bfloat16
F32 = jnp.float32
AXES = ("seq", "tensor")
SY = SX = 4
SZ = 8
FEAT = 128
EXTRA = 16


def pairs(move):
    table = []
    for z in range(SZ):
        for c in range(2):
            for y in range(SY):
                for x in range(SX):
                    z2, c2, y2, x2 = move(z, c, y, x)
                    target = ((z2 % SZ) * 2 + c2) * 16 + (y2 % SY) * 4 + x2 % SX
                    table.append(((z * 2 + c) * 16 + y * 4 + x, target))
    return table


def first(d):
    return pairs(lambda z, c, y, x: (z, c, y + (d if c else 0), x + (0 if c else d)))


def second(d):
    return pairs(lambda z, c, y, x: (z, c, y + (0 if c else d), x + (d if c else 0)))


def along_z(d):
    return pairs(lambda z, c, y, x: (z + d, c, y, x))


SWAP = pairs(lambda z, c, y, x: (z, 1 - c, y, x))
PARTNER = pairs(lambda z, c, y, x: (z + (1 if (z + c) % 2 == 0 else -1), c, y, x))


def send(value, table):
    return lax.ppermute(value, AXES, table)


def block_ids(core, y0, x0):
    ids = []
    for j in (0, -1, 1, 2):
        for i in (0, -1, 1, 2):
            a = (y0 + j) % 4 * 4 + (x0 + i) % 4
            b = (y0 + i) % 4 * 4 + (x0 + j) % 4
            ids.append(jnp.where(core == 0, a, b))
    return ids


def block_body(groups, operands, has_acc, last, *refs):
    refs = list(refs)
    take = lambda n: [refs.pop(0) for _ in range(n)]
    inner = any(g[3] for g in groups)
    outer = any(g[4] for g in groups)
    (ids,) = take(1)
    stacks = take(operands)
    w = take(1)[0] if inner else None
    normed = take(1)[0] if outer else None
    acc_in = take(1)[0] if has_acc else None
    if last:
        weight, normalized = take(2)
    gn = take(1)[0] if inner else None
    mine, other = take(2) if outer else (None, None)
    stat, gain_ref = take(2) if last else (None, None)
    xs, sx = take(2)
    if inner:
        ws, acc, sw, sg = take(4)
    if outer:
        nv, go, sn, so = take(4)
    if has_acc:
        (sa,) = take(1)
    if last:
        pv, sp = take(2)
    tok = xs.shape[1]
    tile = 512
    tiles = tok // tile

    def feed(g):
        members, base, chunk, with_w, _ = groups[g]
        out = []
        for k in range(4):
            n = 4 * g + k
            ref, index = members[k]
            out.append(
                pltpu.make_async_copy(stacks[ref].at[index], xs.at[g, :, pl.ds(k * FEAT, FEAT)], sx.at[n])
            )
            if with_w:
                row = pl.multiple_of(ids[base + k] * (2 * FEAT) + chunk * FEAT, FEAT)
                out.append(
                    pltpu.make_async_copy(w.at[pl.ds(row, FEAT), :], ws.at[g, pl.ds(k * FEAT, FEAT), :], sw.at[n])
                )
        for copy in out:
            copy.start()
        return out

    waiting = {}
    if outer:
        cn = pltpu.make_async_copy(normed, nv, sn)
        cn.start()
        normed_waited = False
    for g in range(min(2, len(groups))):
        waiting[g] = feed(g)
    if has_acc:
        ca = pltpu.make_async_copy(acc_in, acc, sa)
        ca.start()
    if last:
        cp = pltpu.make_async_copy(normalized, pv, sp)
        cp.start()
    done = []
    slot = 0
    for g, (_, base, chunk, with_w, with_n) in enumerate(groups):
        for copy in waiting[g]:
            copy.wait()
        if g + 2 < len(groups):
            waiting[g + 2] = feed(g + 2)
        if with_n:
            if not normed_waited:
                cn.wait()
                normed_waited = True
            go[slot] = lax.dot_general(
                xs[g], nv[...], (((0,), (0,)), ((), ())), preferred_element_type=F32
            )
            for k in range(4):
                place = ids[16 + base + k]
                piece = go.at[slot, pl.ds(k * FEAT, FEAT), :]
                sem = so.at[4 * slot + k]
                row = pl.multiple_of(place % SZ * FEAT, FEAT)

                @pl.when(place < SZ)
                def _():
                    pltpu.make_async_copy(piece, mine.at[pl.ds(row, FEAT), :], sem).start()

                @pl.when(place >= SZ)
                def _():
                    pltpu.make_async_copy(piece, other.at[pl.ds(row, FEAT), :], sem).start()

                done.append(pltpu.make_async_copy(piece, mine.at[pl.ds(0, FEAT), :], sem))
            slot += 1
        if with_w:
            if g == 0 and has_acc:
                ca.wait()
            for t in range(tiles):
                rows = pl.ds(t * tile, tile)
                part = jnp.dot(xs[g, rows, :], ws[g], preferred_element_type=F32)
                if g == 0 and not has_acc:
                    acc[rows, :] = part
                else:
                    acc[rows, :] += part
                if g == len(groups) - 1:
                    out = pltpu.make_async_copy(acc.at[rows, :], gn.at[rows, :], sg.at[t])
                    out.start()
                    done.append(out)
    if last:
        cp.wait()
        gain = jnp.zeros((1, acc.shape[1]), F32)
        for t in range(tok // 128):
            rows = pl.ds(t * 128, 128)
            q = acc[rows, :] * pv[rows, :]
            gain += jnp.sum(q, axis=0, keepdims=True)
            q = q * weight[...]
            folded = q[:, 0:128] + q[:, 128:256] + q[:, 256:384] + q[:, 384:512]
            stat[:, pl.ds(t * 128, 128)] = jnp.sum(folded.T, axis=0, keepdims=True)
        gain_ref[...] = jnp.broadcast_to(gain, gain_ref.shape)
    for copy in done:
        copy.wait()


def block_kernel(name, ids, stacks, groups, w=None, normed=None, acc=None, ends=None):
    tok, ch = 1536, 512
    inner, outer = w is not None, normed is not None
    count = len(groups)
    outers = sum(g[4] for g in groups)
    has_acc, last = acc is not None, ends is not None
    anyspace = pl.BlockSpec(memory_space=pl.ANY)
    whole = pl.BlockSpec(memory_space=pltpu.VMEM)
    in_specs = [pl.BlockSpec(memory_space=pltpu.SMEM)] + [anyspace] * len(stacks)
    args = [ids, *stacks]
    dma = lambda n: pltpu.SemaphoreType.DMA((n,))
    scratch = [pltpu.VMEM((count, tok, 4 * FEAT), BF), dma(4 * count)]
    out_shape = []
    if inner:
        args.append(w)
        in_specs.append(anyspace)
        scratch += [
            pltpu.VMEM((count, 4 * FEAT, ch), BF), pltpu.VMEM((tok, ch), F32), dma(4 * count), dma(tok // 512),
        ]
        out_shape.append(jax.ShapeDtypeStruct((tok, ch), F32))
    if outer:
        args.append(normed)
        in_specs.append(anyspace)
        scratch += [
            pltpu.VMEM((tok, ch), BF), pltpu.VMEM((outers, 4 * FEAT, ch), F32),
            pltpu.SemaphoreType.DMA(()), dma(4 * outers),
        ]
        out_shape += [jax.ShapeDtypeStruct((SZ * FEAT, ch), F32)] * 2
    out_specs = [anyspace] * len(out_shape)
    if has_acc:
        in_specs.append(anyspace)
        args.append(acc)
        scratch.append(pltpu.SemaphoreType.DMA(()))
    if last:
        args += list(ends)
        in_specs += [whole, anyspace]
        out_shape += [jax.ShapeDtypeStruct((1, tok), F32), jax.ShapeDtypeStruct((8, ch), F32)]
        out_specs += [whole, whole]
        scratch += [pltpu.VMEM((tok, ch), F32), pltpu.SemaphoreType.DMA(())]
    work = 8_000_000_000 * sum(g[3] + g[4] for g in groups)
    return pl.pallas_call(
        lambda *refs: block_body(groups, len(stacks), has_acc, last, *refs),
        out_shape=tuple(out_shape),
        in_specs=in_specs,
        out_specs=tuple(out_specs),
        scratch_shapes=scratch,
        compiler_params=pltpu.CompilerParams(vmem_limit_bytes=48 * 1024 * 1024),
        cost_estimate=pl.CostEstimate(flops=work, bytes_accessed=24_000_000 * count, transcendentals=0),
        name=name,
    )(*args)


def split(value):
    high = value.astype(BF)
    rest = value - high.astype(F32)
    middle = rest.astype(BF)
    return high, middle, (rest - middle.astype(F32)).astype(BF)


def mix_body(keep, got, mate, own, gain, *outs):
    half = 4 * FEAT
    total = mate[...][half:, :] + got[...][half:, :]
    gain[...] = total
    wide = jnp.concatenate([total, jnp.zeros_like(total)], axis=0)
    high, middle, low = split(wide)
    row = lax.broadcasted_iota(jnp.int32, wide.shape, 0)
    tail = jnp.where(row == 0, high.astype(F32), 0.0)
    tail = jnp.where(row == 1, middle.astype(F32), tail)
    tail = jnp.where(row == 2, low.astype(F32), tail).astype(BF)
    for m, out in ((0, own), (2, outs[0]), (1, outs[1]), (3, outs[2])):
        rows = slice(m * FEAT, m * FEAT + FEAT)
        value = keep[rows, :] + got[rows, :]
        if m == 0:
            out[...] = value
        else:
            out[0:FEAT, :] = value.astype(BF)
            out[FEAT : FEAT + EXTRA, :] = tail


def mix(keep, got, mate):
    ch = keep.shape[1]
    whole = pl.BlockSpec(memory_space=pltpu.VMEM)
    return pl.pallas_call(
        mix_body,
        out_shape=(jax.ShapeDtypeStruct((FEAT, ch), F32), jax.ShapeDtypeStruct((8, ch), F32))
        + (jax.ShapeDtypeStruct((FEAT + EXTRA, ch), BF),) * 3,
        in_specs=[whole] * 3,
        out_specs=(whole,) * 5,
        name="mix",
    )(keep, got, mate)


def finish_body(own1, own2, gain, a1, b1, c1, a2, b2, c2, rows, total):
    rows[0:FEAT, :] = own1[...] + a1[...].astype(F32) + b1[...].astype(F32) + c1[...].astype(F32)
    rows[FEAT : 2 * FEAT, :] = own2[...] + sum(v[0:FEAT, :].astype(F32) for v in (a2, b2, c2))
    extra = sum(v[FEAT : FEAT + EXTRA, :].astype(F32) for v in (a2, b2, c2))
    total[...] = gain[0:1, :] + jnp.sum(extra, axis=0, keepdims=True)


def finish(own1, own2, gain, gots1, gots2):
    ch = own1.shape[1]
    whole = pl.BlockSpec(memory_space=pltpu.VMEM)
    return pl.pallas_call(
        finish_body,
        out_shape=(jax.ShapeDtypeStruct((2 * FEAT, ch), F32), jax.ShapeDtypeStruct((1, ch), F32)),
        in_specs=[whole] * 9,
        out_specs=(whole, whole),
        name="finish",
    )(own1, own2, gain, *gots1, *gots2)


def all_stats(value):
    spread = jnp.broadcast_to(value.reshape(1, -1), (16, value.size))
    return jnp.sum(lax.all_to_all(spread, "tensor", 0, 0, tiled=True), axis=0)


def local(hidden_states, gate_values, norm_weight, out_weight, out_grad):
    seq = lax.axis_index("seq")
    place = lax.axis_index("tensor")
    core, z0 = seq % 2, seq // 2
    z1 = (z0 + jnp.where((z0 + core) % 2 == 0, 1, -1)) % SZ
    near = lambda value: [value] + [send(value, first(d)) for d in (1, -1, 2)]
    names = block_ids(core, place // 4, place % 4)
    slots = []
    for b in names:
        z = b // 2
        far = (z - z0) % 2
        side = b % 2
        partner = (z0 + jnp.where((z0 + side) % 2 == 0, 1, -1)) % SZ
        slot = far * 4 + (z - jnp.where(far == 0, z0, partner)) % SZ // 2
        slots.append(jnp.where(side == core, 0, SZ) + slot)
    ids = jnp.stack(names + slots).astype(jnp.int32)

    def halves(c):
        cut = [v[:, c * FEAT : (c + 1) * FEAT] for v in blocks]
        return jnp.stack(cut[:2]), jnp.stack(cut[2:])

    def ahead(a, b):
        ra, lb = send(a, second(1)), send(b, second(-1))
        rb, la = send(b, second(1)), send(a, second(-1))
        return ra, rb, la, lb

    def further(ra, rb, la, lb):
        return send(ra, second(1)), send(lb, second(-1))

    blocks = near(out_grad)

    gate_wide = gate_values.astype(F32)
    sigmoid_gate = jax.nn.sigmoid(gate_wide)
    gate_silu = gate_wide * sigmoid_gate
    hidden_wide = hidden_states.astype(F32)
    gated = hidden_wide * gate_silu
    squares = all_stats(jnp.sum(gated * gated, axis=-1))
    blocks, squares = lax.optimization_barrier((blocks, squares))
    inverse_rms = (1.0 / jnp.sqrt(squares / DI + 1e-05))[:, None]
    normalized = gated * inverse_rms
    normed = (normalized * norm_weight).astype(BF)

    pair1 = halves(0)
    ahead1 = ahead(*pair1)
    far1 = further(*ahead1)
    pair2, _ = lax.optimization_barrier((halves(1), (ahead1[1], ahead1[2])))
    ahead2 = ahead(*pair2)
    far2 = further(*ahead2)
    set1, set2 = pair1 + ahead1 + far1, tuple(pair2) + ahead2 + far2

    half = 4 * FEAT
    piece = lambda v, m: v[m * FEAT : (m + 1) * FEAT]

    def grouped(count, chunk, with_w, with_n):
        return [([(2 * k + i // 2, i % 2) for i in range(4)], 4 * k, chunk, with_w, with_n) for k in range(count)]

    mine1, other1 = block_kernel("outer1", ids, set1, grouped(4, 0, 0, 1), None, normed)
    came1 = send(other1, SWAP)
    (grad,) = block_kernel("inner1", ids, set1, grouped(4, 0, 1, 0), out_weight)
    mate1 = (mine1[half:] + came1[half:]).astype(BF)
    keep1 = mine1[:half] + came1[:half]
    mate1, keep1, ids2, grad = lax.optimization_barrier((mate1, keep1, ids, grad))
    got1 = send(mate1, PARTNER)
    mine2, other2 = block_kernel("outer2", ids2, set2, grouped(4, 1, 0, 1), None, normed)
    came2 = send(other2, SWAP)
    grad, mine2, got1 = lax.optimization_barrier((grad, mine2, got1))
    grad_normed, stat, gain = block_kernel(
        "inner2", ids, set2, grouped(4, 1, 1, 0), out_weight, None, grad, (norm_weight[None], normalized)
    )
    gain = gain + send(gain, SWAP)
    sum1 = keep1 + got1.astype(F32)
    outs1 = [piece(sum1, m).astype(BF) for m in (2, 1, 3)]
    mate2 = mine2[half:] + came2[half:]
    keep2 = mine2[:half] + came2[:half]
    mate2, keep2, gain, outs1, stat = lax.optimization_barrier((mate2, keep2, gain, outs1, stat))
    mate2 = jnp.concatenate([mate2, gain])
    got2 = send(mate2, PARTNER)
    gots1 = [send(block, along_z(d)) for block, d in zip(outs1, (4, 2, -2))]
    own2, gain, *outs2 = mix(keep2, got2, mate2)
    products = all_stats(stat)
    outs2, products, gots1 = lax.optimization_barrier((outs2, products, gots1))
    gots2 = [send(block, along_z(d)) for block, d in zip(outs2, (4, 2, -2))]
    rows, gain = finish(piece(sum1, 0), own2, gain, gots1, gots2)

    weighted = grad_normed * norm_weight
    grad_gated = inverse_rms * (weighted - normalized * (products / DI)[:, None])
    grad_hidden = (grad_gated * gate_silu).astype(BF)
    grad_gate = (
        grad_gated * hidden_wide * sigmoid_gate * (1.0 + gate_wide * (1.0 - sigmoid_gate))
    ).astype(BF)
    return grad_hidden, grad_gate, rows, gain[0]


def solution(mesh):
    return jax.shard_map(
        local,
        mesh=mesh,
        in_specs=(
            P("seq", "tensor"),
            P("seq", "tensor"),
            P("tensor"),
            P(None, "tensor"),
            P("seq", "tensor"),
        ),
        out_specs=(P("seq", "tensor"), P("seq", "tensor"), P("seq", "tensor"), P("tensor")),
        check_vma=False,
    )
```

```python
import jax
import jax.numpy as jnp
from jax import lax
from jax.experimental import pallas as pl
from jax.experimental.pallas import tpu as pltpu
from jax.sharding import PartitionSpec as P

DI = 8192
BF = jnp.bfloat16
F32 = jnp.float32
AXES = ("seq", "tensor")
SY = SX = 4
SZ = 8
FEAT = 128


def pairs(move):
    table = []
    for z in range(SZ):
        for c in range(2):
            for y in range(SY):
                for x in range(SX):
                    z2, c2, y2, x2 = move(z, c, y, x)
                    target = ((z2 % SZ) * 2 + c2) * 16 + (y2 % SY) * 4 + x2 % SX
                    table.append(((z * 2 + c) * 16 + y * 4 + x, target))
    return table


def first(d):
    return pairs(lambda z, c, y, x: (z, c, y + (d if c else 0), x + (0 if c else d)))


def second(d):
    return pairs(lambda z, c, y, x: (z, c, y + (0 if c else d), x + (d if c else 0)))


def along_z(d):
    return pairs(lambda z, c, y, x: (z + d, c, y, x))


SWAP = pairs(lambda z, c, y, x: (z, 1 - c, y, x))
PARTNER = pairs(lambda z, c, y, x: (z + (1 if (z + c) % 2 == 0 else -1), c, y, x))


def send(value, table):
    return lax.ppermute(value, AXES, table)


def block_ids(core, y0, x0):
    ids = []
    for j in (0, -1, 1, 2):
        for i in (0, -1, 1, 2):
            a = (y0 + j) % 4 * 4 + (x0 + i) % 4
            b = (y0 + i) % 4 * 4 + (x0 + j) % 4
            ids.append(jnp.where(core == 0, a, b))
    return ids


def block_body(groups, operands, has_acc, last, *refs):
    refs = list(refs)
    take = lambda n: [refs.pop(0) for _ in range(n)]
    inner = any(g[3] for g in groups)
    outer = any(g[4] for g in groups)
    (ids,) = take(1)
    stacks = take(operands)
    w = take(1)[0] if inner else None
    normed = take(1)[0] if outer else None
    acc_in = take(1)[0] if has_acc else None
    if last:
        weight, normalized = take(2)
    gn = take(1)[0] if inner else None
    mine, other = take(2) if outer else (None, None)
    stat, gain_ref = take(2) if last else (None, None)
    xs, sx = take(2)
    if inner:
        ws, acc, sw, sg = take(4)
    if outer:
        nv, go, sn, so = take(4)
    if has_acc:
        (sa,) = take(1)
    if last:
        pv, sp = take(2)
    tok = xs.shape[1]
    tile = 512
    tiles = tok // tile

    def feed(g):
        members, base, chunk, with_w, _ = groups[g]
        out = []
        for k in range(4):
            n = 4 * g + k
            ref, index = members[k]
            out.append(
                pltpu.make_async_copy(stacks[ref].at[index], xs.at[g, :, pl.ds(k * FEAT, FEAT)], sx.at[n])
            )
            if with_w:
                row = pl.multiple_of(ids[base + k] * (2 * FEAT) + chunk * FEAT, FEAT)
                out.append(
                    pltpu.make_async_copy(w.at[pl.ds(row, FEAT), :], ws.at[g, pl.ds(k * FEAT, FEAT), :], sw.at[n])
                )
        for copy in out:
            copy.start()
        return out

    waiting = {}
    if outer:
        cn = pltpu.make_async_copy(normed, nv, sn)
        cn.start()
        normed_waited = False
    for g in range(min(2, len(groups))):
        waiting[g] = feed(g)
    if has_acc:
        ca = pltpu.make_async_copy(acc_in, acc, sa)
        ca.start()
    if last:
        cp = pltpu.make_async_copy(normalized, pv, sp)
        cp.start()
    done = []
    slot = 0
    for g, (_, base, chunk, with_w, with_n) in enumerate(groups):
        for copy in waiting[g]:
            copy.wait()
        if g + 2 < len(groups):
            waiting[g + 2] = feed(g + 2)
        if with_n:
            if not normed_waited:
                cn.wait()
                normed_waited = True
            go[slot] = lax.dot_general(
                xs[g], nv[...], (((0,), (0,)), ((), ())), preferred_element_type=F32
            )
            for k in range(4):
                place = ids[16 + base + k]
                piece = go.at[slot, pl.ds(k * FEAT, FEAT), :]
                sem = so.at[4 * slot + k]
                row = pl.multiple_of(place % SZ * FEAT, FEAT)

                @pl.when(place < SZ)
                def _():
                    pltpu.make_async_copy(piece, mine.at[pl.ds(row, FEAT), :], sem).start()

                @pl.when(place >= SZ)
                def _():
                    pltpu.make_async_copy(piece, other.at[pl.ds(row, FEAT), :], sem).start()

                done.append(pltpu.make_async_copy(piece, mine.at[pl.ds(0, FEAT), :], sem))
            slot += 1
        if with_w:
            if g == 0 and has_acc:
                ca.wait()
            for t in range(tiles):
                rows = pl.ds(t * tile, tile)
                part = jnp.dot(xs[g, rows, :], ws[g], preferred_element_type=F32)
                if g == 0 and not has_acc:
                    acc[rows, :] = part
                else:
                    acc[rows, :] += part
                if g == len(groups) - 1:
                    out = pltpu.make_async_copy(acc.at[rows, :], gn.at[rows, :], sg.at[t])
                    out.start()
                    done.append(out)
    if last:
        cp.wait()
        gain = jnp.zeros((1, acc.shape[1]), F32)
        for t in range(tok // 128):
            rows = pl.ds(t * 128, 128)
            q = acc[rows, :] * pv[rows, :]
            gain += jnp.sum(q, axis=0, keepdims=True)
            q = q * weight[...]
            folded = q[:, 0:128] + q[:, 128:256] + q[:, 256:384] + q[:, 384:512]
            stat[:, pl.ds(t * 128, 128)] = jnp.sum(folded.T, axis=0, keepdims=True)
        gain_ref[...] = jnp.broadcast_to(gain, gain_ref.shape)
    for copy in done:
        copy.wait()


def block_kernel(name, ids, stacks, groups, w=None, normed=None, acc=None, ends=None):
    tok, ch = 1536, 512
    inner, outer = w is not None, normed is not None
    count = len(groups)
    outers = sum(g[4] for g in groups)
    has_acc, last = acc is not None, ends is not None
    anyspace = pl.BlockSpec(memory_space=pl.ANY)
    whole = pl.BlockSpec(memory_space=pltpu.VMEM)
    in_specs = [pl.BlockSpec(memory_space=pltpu.SMEM)] + [anyspace] * len(stacks)
    args = [ids, *stacks]
    dma = lambda n: pltpu.SemaphoreType.DMA((n,))
    scratch = [pltpu.VMEM((count, tok, 4 * FEAT), BF), dma(4 * count)]
    out_shape = []
    if inner:
        args.append(w)
        in_specs.append(anyspace)
        scratch += [
            pltpu.VMEM((count, 4 * FEAT, ch), BF), pltpu.VMEM((tok, ch), F32), dma(4 * count), dma(tok // 512),
        ]
        out_shape.append(jax.ShapeDtypeStruct((tok, ch), F32))
    if outer:
        args.append(normed)
        in_specs.append(anyspace)
        scratch += [
            pltpu.VMEM((tok, ch), BF), pltpu.VMEM((outers, 4 * FEAT, ch), F32),
            pltpu.SemaphoreType.DMA(()), dma(4 * outers),
        ]
        out_shape += [jax.ShapeDtypeStruct((SZ * FEAT, ch), F32)] * 2
    out_specs = [anyspace] * len(out_shape)
    if has_acc:
        in_specs.append(anyspace)
        args.append(acc)
        scratch.append(pltpu.SemaphoreType.DMA(()))
    if last:
        args += list(ends)
        in_specs += [whole, anyspace]
        out_shape += [jax.ShapeDtypeStruct((1, tok), F32), jax.ShapeDtypeStruct((8, ch), F32)]
        out_specs += [whole, whole]
        scratch += [pltpu.VMEM((tok, ch), F32), pltpu.SemaphoreType.DMA(())]
    work = 8_000_000_000 * sum(g[3] + g[4] for g in groups)
    return pl.pallas_call(
        lambda *refs: block_body(groups, len(stacks), has_acc, last, *refs),
        out_shape=tuple(out_shape),
        in_specs=in_specs,
        out_specs=tuple(out_specs),
        scratch_shapes=scratch,
        compiler_params=pltpu.CompilerParams(vmem_limit_bytes=48 * 1024 * 1024),
        cost_estimate=pl.CostEstimate(flops=work, bytes_accessed=24_000_000 * count, transcendentals=0),
        name=name,
    )(*args)


def mix_body(mine1, came1, got1, mine2, came2, got2, own, *outs):
    for c, (mine, came, got) in enumerate(((mine1, came1, got1), (mine2, came2, got2))):
        for m, out in ((0, own), (2, outs[0]), (1, outs[1]), (3, outs[2])):
            rows = slice(m * FEAT, m * FEAT + FEAT)
            value = mine[rows, :] + came[rows, :] + got[rows, :].astype(F32)
            out[c * FEAT : (c + 1) * FEAT, :] = value.astype(out.dtype)


def mix(mine1, came1, got1, mine2, came2, got2):
    ch = mine1.shape[1]
    part = pl.BlockSpec((4 * FEAT, ch), lambda i: (0, 0))
    whole = pl.BlockSpec((2 * FEAT, ch), lambda i: (0, 0))
    return pl.pallas_call(
        mix_body,
        grid=(1,),
        out_shape=(jax.ShapeDtypeStruct((2 * FEAT, ch), F32),) + (jax.ShapeDtypeStruct((2 * FEAT, ch), BF),) * 3,
        in_specs=[part] * 6,
        out_specs=(whole,) * 4,
        cost_estimate=pl.CostEstimate(flops=4_000_000, bytes_accessed=8_000_000, transcendentals=0),
        name="mix",
    )(mine1, came1, got1, mine2, came2, got2)


def parts_of(value, axis):
    spread = jnp.broadcast_to(value.reshape(1, -1), (16, value.size))
    return lax.all_to_all(spread, axis, 0, 0, tiled=True)


def total(value, axis):
    return jnp.sum(parts_of(value, axis), axis=0)


def last_body(hidden, gate, grad, normalized, weight, inverse, products, grad_hidden, grad_gate):
    for t in range(hidden.shape[0] // 128):
        part = slice(t * 128, t * 128 + 128)
        row = jnp.sum(products[:, part], axis=0, keepdims=True) / DI
        mean = jnp.broadcast_to(row, (128, 128)).T
        scale = jnp.broadcast_to(inverse[:, part], (128, 128)).T
        for k in range(hidden.shape[1] // 128):
            lanes = slice(k * 128, k * 128 + 128)
            g = gate[part, lanes].astype(F32)
            sigmoid = 0.5 + 0.5 * jnp.tanh(0.5 * g)
            d = scale * (grad[part, lanes] * weight[:, lanes] - normalized[part, lanes] * mean)
            grad_hidden[part, lanes] = (d * (g * sigmoid)).astype(BF)
            slope = sigmoid * (1.0 + g * (1.0 - sigmoid))
            grad_gate[part, lanes] = (d * hidden[part, lanes].astype(F32) * slope).astype(BF)


def last(hidden, gate, grad, normalized, weight, inverse, products):
    tok, ch = hidden.shape
    tile = 512
    wide = pl.BlockSpec((tile, ch), lambda i: (i, 0))
    return pl.pallas_call(
        last_body,
        grid=(tok // tile,),
        out_shape=(jax.ShapeDtypeStruct((tok, ch), BF),) * 2,
        in_specs=[
            wide, wide, wide, wide,
            pl.BlockSpec((1, ch), lambda i: (0, 0)),
            pl.BlockSpec((1, tile), lambda i: (0, i)),
            pl.BlockSpec((16, tile), lambda i: (0, i)),
        ],
        out_specs=(wide, wide),
        cost_estimate=pl.CostEstimate(flops=1_000, bytes_accessed=1_000, transcendentals=0),
        name="last",
    )(hidden, gate, grad, normalized, weight, inverse, products)


def local(hidden_states, gate_values, norm_weight, out_weight, out_grad):
    seq = lax.axis_index("seq")
    place = lax.axis_index("tensor")
    core, z0 = seq % 2, seq // 2
    z1 = (z0 + jnp.where((z0 + core) % 2 == 0, 1, -1)) % SZ
    near = lambda value: [value] + [send(value, first(d)) for d in (1, -1, 2)]
    names = block_ids(core, place // 4, place % 4)
    slots = []
    for b in names:
        z = b // 2
        far = (z - z0) % 2
        side = b % 2
        partner = (z0 + jnp.where((z0 + side) % 2 == 0, 1, -1)) % SZ
        slot = far * 4 + (z - jnp.where(far == 0, z0, partner)) % SZ // 2
        slots.append(jnp.where(side == core, 0, SZ) + slot)
    ids = jnp.stack(names + slots).astype(jnp.int32)

    def gather(value):
        stack = jnp.stack([value] + [send(value, first(d)) for d in (1, -1, 2)])
        right, left = send(stack, second(1)), send(stack, second(-1))
        return stack, right, left, send(right[:2], second(1)), send(left[2:], second(-1))

    set1 = gather(out_grad[:, :FEAT])
    set2 = gather(out_grad[:, FEAT:])

    gate_wide = gate_values.astype(F32)
    sigmoid_gate = jax.nn.sigmoid(gate_wide)
    gate_silu = gate_wide * sigmoid_gate
    hidden_wide = hidden_states.astype(F32)
    gated = hidden_wide * gate_silu
    squares = total(jnp.sum(gated * gated, axis=-1), "tensor")
    inverse_rms = 1.0 / jnp.sqrt(squares / DI + 1e-05)
    normalized = gated * inverse_rms[:, None]
    normed = (normalized * norm_weight).astype(BF)

    def grouped(operand, chunk, with_w, with_n):
        n = operand
        parts = [[(n + j, k) for k in range(4)] for j in range(3)] + [[(n + 3, 0), (n + 3, 1), (n + 4, 0), (n + 4, 1)]]
        return [(parts[k], 4 * k, chunk, with_w, with_n) for k in range(4)]

    half = 4 * FEAT
    mine1, other1 = block_kernel("outer1", ids, set1, grouped(0, 0, 0, 1), None, normed)
    came1 = send(other1, SWAP)
    mine2, other2 = block_kernel("outer2", ids, set2, grouped(0, 1, 0, 1), None, normed)
    came2 = send(other2, SWAP)
    mate1 = (mine1[half:] + came1[half:]).astype(BF)
    mate2 = (mine2[half:] + came2[half:]).astype(BF)
    mate1, mate2, ids1 = lax.optimization_barrier((mate1, mate2, ids))
    got1, got2 = send(mate1, PARTNER), send(mate2, PARTNER)
    grad_normed, stat, gain = block_kernel(
        "inner", ids1, set1 + set2, grouped(0, 0, 1, 0) + grouped(5, 1, 1, 0), out_weight, None, None,
        (norm_weight[None], normalized),
    )
    got1, got2, stat = lax.optimization_barrier((got1, got2, stat))
    own, *outs = mix(mine1, came1, got1, mine2, came2, got2)
    rows = own
    for block, d in zip((outs[1], outs[2], outs[0]), (2, -2, 4)):
        rows = rows + send(block, along_z(d)).astype(F32)
    products = parts_of(stat, "tensor")
    grad_hidden, grad_gate = last(
        hidden_states, gate_values, grad_normed, normalized, norm_weight[None], inverse_rms[None], products
    )
    gain, _ = lax.optimization_barrier((gain[0], products))
    grad_norm_weight = total(gain, "seq")
    return grad_hidden, grad_gate, rows, grad_norm_weight


def solution(mesh):
    return jax.shard_map(
        local,
        mesh=mesh,
        in_specs=(
            P("seq", "tensor"),
            P("seq", "tensor"),
            P("tensor"),
            P(None, "tensor"),
            P("seq", "tensor"),
        ),
        out_specs=(P("seq", "tensor"), P("seq", "tensor"), P("seq", "tensor"), P("tensor")),
        check_vma=False,
    )
```

```python
import jax
import jax.numpy as jnp
from jax import lax
from jax.experimental import pallas as pl
from jax.experimental.pallas import tpu as pltpu
from jax.sharding import PartitionSpec as P

DI = 8192
BF = jnp.bfloat16
F32 = jnp.float32
AXES = ("seq", "tensor")
SY = SX = 4
SZ = 8
FEAT = 128


def pairs(move):
    table = []
    for z in range(SZ):
        for c in range(2):
            for y in range(SY):
                for x in range(SX):
                    z2, c2, y2, x2 = move(z, c, y, x)
                    target = ((z2 % SZ) * 2 + c2) * 16 + (y2 % SY) * 4 + x2 % SX
                    table.append(((z * 2 + c) * 16 + y * 4 + x, target))
    return table


def first(d):
    return pairs(lambda z, c, y, x: (z, c, y + (d if c else 0), x + (0 if c else d)))


def second(d):
    return pairs(lambda z, c, y, x: (z, c, y + (0 if c else d), x + (d if c else 0)))


def along_z(d):
    return pairs(lambda z, c, y, x: (z + d, c, y, x))


SWAP = pairs(lambda z, c, y, x: (z, 1 - c, y, x))
PARTNER = pairs(lambda z, c, y, x: (z + (1 if (z + c) % 2 == 0 else -1), c, y, x))


def send(value, table):
    return lax.ppermute(value, AXES, table)


def block_ids(core, y0, x0):
    ids = []
    for j in (0, -1, 1, 2):
        for i in (0, -1, 1, 2):
            a = (y0 + j) % 4 * 4 + (x0 + i) % 4
            b = (y0 + i) % 4 * 4 + (x0 + j) % 4
            ids.append(jnp.where(core == 0, a, b))
    return ids


def block_body(groups, operands, has_acc, last, *refs):
    refs = list(refs)
    take = lambda n: [refs.pop(0) for _ in range(n)]
    inner = any(g[3] for g in groups)
    outer = any(g[4] for g in groups)
    (ids,) = take(1)
    stacks = take(operands)
    w = take(1)[0] if inner else None
    normed = take(1)[0] if outer else None
    acc_in = take(1)[0] if has_acc else None
    if last:
        weight, normalized = take(2)
    gn = take(1)[0] if inner else None
    mine, other = take(2) if outer else (None, None)
    stat, gain_ref = take(2) if last else (None, None)
    xs, sx = take(2)
    if inner:
        ws, acc, sw, sg = take(4)
    if outer:
        nv, go, sn, so = take(4)
    if has_acc:
        (sa,) = take(1)
    if last:
        pv, sp = take(2)
    tok = xs.shape[1]
    tile = 512
    tiles = tok // tile

    def feed(g):
        members, base, chunk, with_w, _ = groups[g]
        out = []
        for k in range(4):
            n = 4 * g + k
            ref, index = members[k]
            out.append(
                pltpu.make_async_copy(stacks[ref].at[index], xs.at[g, :, pl.ds(k * FEAT, FEAT)], sx.at[n])
            )
            if with_w:
                row = pl.multiple_of(ids[base + k] * (2 * FEAT) + chunk * FEAT, FEAT)
                out.append(
                    pltpu.make_async_copy(w.at[pl.ds(row, FEAT), :], ws.at[g, pl.ds(k * FEAT, FEAT), :], sw.at[n])
                )
        for copy in out:
            copy.start()
        return out

    waiting = {}
    if outer:
        cn = pltpu.make_async_copy(normed, nv, sn)
        cn.start()
        normed_waited = False
    for g in range(min(2, len(groups))):
        waiting[g] = feed(g)
    if has_acc:
        ca = pltpu.make_async_copy(acc_in, acc, sa)
        ca.start()
    if last:
        cp = pltpu.make_async_copy(normalized, pv, sp)
        cp.start()
    done = []
    slot = 0
    for g, (_, base, chunk, with_w, with_n) in enumerate(groups):
        for copy in waiting[g]:
            copy.wait()
        if g + 2 < len(groups):
            waiting[g + 2] = feed(g + 2)
        if with_n:
            if not normed_waited:
                cn.wait()
                normed_waited = True
            go[slot] = lax.dot_general(
                xs[g], nv[...], (((0,), (0,)), ((), ())), preferred_element_type=F32
            )
            for k in range(4):
                place = ids[16 + base + k]
                piece = go.at[slot, pl.ds(k * FEAT, FEAT), :]
                sem = so.at[4 * slot + k]
                row = pl.multiple_of(place % SZ * FEAT, FEAT)

                @pl.when(place < SZ)
                def _():
                    pltpu.make_async_copy(piece, mine.at[pl.ds(row, FEAT), :], sem).start()

                @pl.when(place >= SZ)
                def _():
                    pltpu.make_async_copy(piece, other.at[pl.ds(row, FEAT), :], sem).start()

                done.append(pltpu.make_async_copy(piece, mine.at[pl.ds(0, FEAT), :], sem))
            slot += 1
        if with_w:
            if g == 0 and has_acc:
                ca.wait()
            for t in range(tiles):
                rows = pl.ds(t * tile, tile)
                part = jnp.dot(xs[g, rows, :], ws[g], preferred_element_type=F32)
                if g == 0 and not has_acc:
                    acc[rows, :] = part
                else:
                    acc[rows, :] += part
                if g == len(groups) - 1:
                    out = pltpu.make_async_copy(acc.at[rows, :], gn.at[rows, :], sg.at[t])
                    out.start()
                    done.append(out)
    if last:
        cp.wait()
        gain = jnp.zeros((1, acc.shape[1]), F32)
        for t in range(tok // 128):
            rows = pl.ds(t * 128, 128)
            q = acc[rows, :] * pv[rows, :]
            gain += jnp.sum(q, axis=0, keepdims=True)
            q = q * weight[...]
            folded = q[:, 0:128] + q[:, 128:256] + q[:, 256:384] + q[:, 384:512]
            stat[:, pl.ds(t * 128, 128)] = jnp.sum(folded.T, axis=0, keepdims=True)
        gain_ref[...] = jnp.broadcast_to(gain, gain_ref.shape)
    for copy in done:
        copy.wait()


def block_kernel(name, ids, stacks, groups, w=None, normed=None, acc=None, ends=None):
    tok, ch = 1536, 512
    inner, outer = w is not None, normed is not None
    count = len(groups)
    outers = sum(g[4] for g in groups)
    has_acc, last = acc is not None, ends is not None
    anyspace = pl.BlockSpec(memory_space=pl.ANY)
    whole = pl.BlockSpec(memory_space=pltpu.VMEM)
    in_specs = [pl.BlockSpec(memory_space=pltpu.SMEM)] + [anyspace] * len(stacks)
    args = [ids, *stacks]
    dma = lambda n: pltpu.SemaphoreType.DMA((n,))
    scratch = [pltpu.VMEM((count, tok, 4 * FEAT), BF), dma(4 * count)]
    out_shape = []
    if inner:
        args.append(w)
        in_specs.append(anyspace)
        scratch += [
            pltpu.VMEM((count, 4 * FEAT, ch), BF), pltpu.VMEM((tok, ch), F32), dma(4 * count), dma(tok // 512),
        ]
        out_shape.append(jax.ShapeDtypeStruct((tok, ch), F32))
    if outer:
        args.append(normed)
        in_specs.append(anyspace)
        scratch += [
            pltpu.VMEM((tok, ch), BF), pltpu.VMEM((outers, 4 * FEAT, ch), F32),
            pltpu.SemaphoreType.DMA(()), dma(4 * outers),
        ]
        out_shape += [jax.ShapeDtypeStruct((SZ * FEAT, ch), F32)] * 2
    out_specs = [anyspace] * len(out_shape)
    if has_acc:
        in_specs.append(anyspace)
        args.append(acc)
        scratch.append(pltpu.SemaphoreType.DMA(()))
    if last:
        args += list(ends)
        in_specs += [whole, anyspace]
        out_shape += [jax.ShapeDtypeStruct((1, tok), F32), jax.ShapeDtypeStruct((8, ch), F32)]
        out_specs += [whole, whole]
        scratch += [pltpu.VMEM((tok, ch), F32), pltpu.SemaphoreType.DMA(())]
    work = 8_000_000_000 * sum(g[3] + g[4] for g in groups)
    return pl.pallas_call(
        lambda *refs: block_body(groups, len(stacks), has_acc, last, *refs),
        out_shape=tuple(out_shape),
        in_specs=in_specs,
        out_specs=tuple(out_specs),
        scratch_shapes=scratch,
        compiler_params=pltpu.CompilerParams(vmem_limit_bytes=48 * 1024 * 1024),
        cost_estimate=pl.CostEstimate(flops=work, bytes_accessed=24_000_000 * count, transcendentals=0),
        name=name,
    )(*args)


def mix_body(mine1, came1, got1, mine2, came2, got2, own, *outs):
    for c, (mine, came, got) in enumerate(((mine1, came1, got1), (mine2, came2, got2))):
        for m, out in ((0, own), (2, outs[0]), (1, outs[1]), (3, outs[2])):
            rows = slice(m * FEAT, m * FEAT + FEAT)
            value = mine[rows, :] + came[rows, :] + got[rows, :].astype(F32)
            out[c * FEAT : (c + 1) * FEAT, :] = value.astype(out.dtype)


def mix(mine1, came1, got1, mine2, came2, got2):
    ch = mine1.shape[1]
    part = pl.BlockSpec((4 * FEAT, ch), lambda i: (0, 0))
    whole = pl.BlockSpec((2 * FEAT, ch), lambda i: (0, 0))
    return pl.pallas_call(
        mix_body,
        grid=(1,),
        out_shape=(jax.ShapeDtypeStruct((2 * FEAT, ch), F32),) + (jax.ShapeDtypeStruct((2 * FEAT, ch), BF),) * 3,
        in_specs=[part] * 6,
        out_specs=(whole,) * 4,
        cost_estimate=pl.CostEstimate(flops=4_000_000, bytes_accessed=8_000_000, transcendentals=0),
        name="mix",
    )(mine1, came1, got1, mine2, came2, got2)


def parts_of(value, axis):
    spread = jnp.broadcast_to(value.reshape(1, -1), (16, value.size))
    return lax.all_to_all(spread, axis, 0, 0, tiled=True)


def total(value, axis):
    return jnp.sum(parts_of(value, axis), axis=0)


def last_body(hidden, gate, grad, normalized, weight, inverse, products, grad_hidden, grad_gate):
    for t in range(hidden.shape[0] // 128):
        part = slice(t * 128, t * 128 + 128)
        row = jnp.sum(products[:, part], axis=0, keepdims=True) / DI
        mean = jnp.broadcast_to(row, (128, 128)).T
        scale = jnp.broadcast_to(inverse[:, part], (128, 128)).T
        for k in range(hidden.shape[1] // 128):
            lanes = slice(k * 128, k * 128 + 128)
            g = gate[part, lanes].astype(F32)
            sigmoid = 0.5 + 0.5 * jnp.tanh(0.5 * g)
            d = scale * (grad[part, lanes] * weight[:, lanes] - normalized[part, lanes] * mean)
            grad_hidden[part, lanes] = (d * (g * sigmoid)).astype(BF)
            slope = sigmoid * (1.0 + g * (1.0 - sigmoid))
            grad_gate[part, lanes] = (d * hidden[part, lanes].astype(F32) * slope).astype(BF)


def last(hidden, gate, grad, normalized, weight, inverse, products):
    tok, ch = hidden.shape
    tile = 512
    wide = pl.BlockSpec((tile, ch), lambda i: (i, 0))
    return pl.pallas_call(
        last_body,
        grid=(tok // tile,),
        out_shape=(jax.ShapeDtypeStruct((tok, ch), BF),) * 2,
        in_specs=[
            wide, wide, wide, wide,
            pl.BlockSpec((1, ch), lambda i: (0, 0)),
            pl.BlockSpec((1, tile), lambda i: (0, i)),
            pl.BlockSpec((16, tile), lambda i: (0, i)),
        ],
        out_specs=(wide, wide),
        cost_estimate=pl.CostEstimate(flops=1_000, bytes_accessed=1_000, transcendentals=0),
        name="last",
    )(hidden, gate, grad, normalized, weight, inverse, products)


def local(hidden_states, gate_values, norm_weight, out_weight, out_grad):
    seq = lax.axis_index("seq")
    place = lax.axis_index("tensor")
    core, z0 = seq % 2, seq // 2
    z1 = (z0 + jnp.where((z0 + core) % 2 == 0, 1, -1)) % SZ
    near = lambda value: [value] + [send(value, first(d)) for d in (1, -1, 2)]
    names = block_ids(core, place // 4, place % 4)
    slots = []
    for b in names:
        z = b // 2
        far = (z - z0) % 2
        side = b % 2
        partner = (z0 + jnp.where((z0 + side) % 2 == 0, 1, -1)) % SZ
        slot = far * 4 + (z - jnp.where(far == 0, z0, partner)) % SZ // 2
        slots.append(jnp.where(side == core, 0, SZ) + slot)
    ids = jnp.stack(names + slots).astype(jnp.int32)

    def gather(value):
        stack = jnp.stack([value] + [send(value, first(d)) for d in (1, -1, 2)])
        right, left = send(stack, second(1)), send(stack, second(-1))
        return stack, right, left, send(right[:2], second(1)), send(left[2:], second(-1))

    set1 = gather(out_grad[:, :FEAT])
    set2 = gather(out_grad[:, FEAT:])

    gate_wide = gate_values.astype(F32)
    sigmoid_gate = jax.nn.sigmoid(gate_wide)
    gate_silu = gate_wide * sigmoid_gate
    hidden_wide = hidden_states.astype(F32)
    gated = hidden_wide * gate_silu
    squares = total(jnp.sum(gated * gated, axis=-1), "tensor")
    inverse_rms = 1.0 / jnp.sqrt(squares / DI + 1e-05)
    normalized = gated * inverse_rms[:, None]
    normed = (normalized * norm_weight).astype(BF)

    def grouped(operand, chunk, with_w, with_n):
        n = operand
        parts = [[(n + j, k) for k in range(4)] for j in range(3)] + [[(n + 3, 0), (n + 3, 1), (n + 4, 0), (n + 4, 1)]]
        return [(parts[k], 4 * k, chunk, with_w, with_n) for k in range(4)]

    half = 4 * FEAT
    mine1, other1 = block_kernel("outer1", ids, set1, grouped(0, 0, 0, 1), None, normed)
    came1 = send(other1, SWAP)
    mine2, other2 = block_kernel("outer2", ids, set2, grouped(0, 1, 0, 1), None, normed)
    came2 = send(other2, SWAP)
    mate1 = (mine1[half:] + came1[half:]).astype(BF)
    mate2 = (mine2[half:] + came2[half:]).astype(BF)
    mate1, mate2, ids1 = lax.optimization_barrier((mate1, mate2, ids))
    got1, got2 = send(mate1, PARTNER), send(mate2, PARTNER)
    grad_normed, stat, gain = block_kernel(
        "inner", ids1, set1 + set2, grouped(0, 0, 1, 0) + grouped(5, 1, 1, 0), out_weight, None, None,
        (norm_weight[None], normalized),
    )
    got1, got2, stat = lax.optimization_barrier((got1, got2, stat))
    own, *outs = mix(mine1, came1, got1, mine2, came2, got2)
    gots = [send(block, along_z(d)) for block, d in zip((outs[1], outs[2], outs[0]), (2, -2, 4))]
    products = parts_of(jnp.tile(stat, (1, 4)), "tensor")
    grad_hidden, grad_gate = last(
        hidden_states, gate_values, grad_normed, normalized, norm_weight[None], inverse_rms[None], products
    )
    gain, _ = lax.optimization_barrier((gain[0], products))
    gains = parts_of(gain, "seq")
    gains, gots = lax.optimization_barrier((gains, gots))
    grad_norm_weight = jnp.sum(gains, axis=0)
    rows = own
    for got in gots:
        rows = rows + got.astype(F32)
    return grad_hidden, grad_gate, rows, grad_norm_weight


def solution(mesh):
    return jax.shard_map(
        local,
        mesh=mesh,
        in_specs=(
            P("seq", "tensor"),
            P("seq", "tensor"),
            P("tensor"),
            P(None, "tensor"),
            P("seq", "tensor"),
        ),
        out_specs=(P("seq", "tensor"), P("seq", "tensor"), P("seq", "tensor"), P("tensor")),
        check_vma=False,
    )
```

```python
import jax
import jax.numpy as jnp
from jax import lax
from jax.experimental import pallas as pl
from jax.experimental.pallas import tpu as pltpu
from jax.sharding import PartitionSpec as P

DI = 8192
BF = jnp.bfloat16
F32 = jnp.float32
AXES = ("seq", "tensor")
SY = SX = 4
SZ = 8
FEAT = 128


def pairs(move):
    table = []
    for z in range(SZ):
        for c in range(2):
            for y in range(SY):
                for x in range(SX):
                    z2, c2, y2, x2 = move(z, c, y, x)
                    target = ((z2 % SZ) * 2 + c2) * 16 + (y2 % SY) * 4 + x2 % SX
                    table.append(((z * 2 + c) * 16 + y * 4 + x, target))
    return table


def first(d):
    return pairs(lambda z, c, y, x: (z, c, y + (d if c else 0), x + (0 if c else d)))


def second(d):
    return pairs(lambda z, c, y, x: (z, c, y + (0 if c else d), x + (d if c else 0)))


def along_z(d):
    return pairs(lambda z, c, y, x: (z + d, c, y, x))


SWAP = pairs(lambda z, c, y, x: (z, 1 - c, y, x))
PARTNER = pairs(lambda z, c, y, x: (z + (1 if (z + c) % 2 == 0 else -1), c, y, x))


def send(value, table):
    return lax.ppermute(value, AXES, table)


def block_ids(core, y0, x0):
    ids = []
    for j in (0, -1, 1, 2):
        for i in (0, -1, 1, 2):
            a = (y0 + j) % 4 * 4 + (x0 + i) % 4
            b = (y0 + i) % 4 * 4 + (x0 + j) % 4
            ids.append(jnp.where(core == 0, a, b))
    return ids


def block_body(groups, operands, has_acc, last, *refs):
    refs = list(refs)
    take = lambda n: [refs.pop(0) for _ in range(n)]
    inner = any(g[3] for g in groups)
    outer = any(g[4] for g in groups)
    (ids,) = take(1)
    stacks = take(operands)
    w = take(1)[0] if inner else None
    normed = take(1)[0] if outer else None
    acc_in = take(1)[0] if has_acc else None
    if last:
        weight, normalized = take(2)
    gn = take(1)[0] if inner else None
    mine, other = take(2) if outer else (None, None)
    stat, gain_ref = take(2) if last else (None, None)
    xs, sx = take(2)
    if inner:
        ws, acc, sw, sg = take(4)
    if outer:
        nv, go, sn, so = take(4)
    if has_acc:
        (sa,) = take(1)
    if last:
        pv, sp = take(2)
    tok = xs.shape[1]
    tile = 512
    tiles = tok // tile

    def feed(g):
        members, base, chunk, with_w, _ = groups[g]
        out = []
        for k in range(4):
            n = 4 * g + k
            ref, index = members[k]
            out.append(
                pltpu.make_async_copy(stacks[ref].at[index], xs.at[g, :, pl.ds(k * FEAT, FEAT)], sx.at[n])
            )
            if with_w:
                row = pl.multiple_of(ids[base + k] * (2 * FEAT) + chunk * FEAT, FEAT)
                out.append(
                    pltpu.make_async_copy(w.at[pl.ds(row, FEAT), :], ws.at[g, pl.ds(k * FEAT, FEAT), :], sw.at[n])
                )
        for copy in out:
            copy.start()
        return out

    waiting = {}
    if outer:
        cn = pltpu.make_async_copy(normed, nv, sn)
        cn.start()
        normed_waited = False
    for g in range(min(2, len(groups))):
        waiting[g] = feed(g)
    if has_acc:
        ca = pltpu.make_async_copy(acc_in, acc, sa)
        ca.start()
    if last:
        cp = pltpu.make_async_copy(normalized, pv, sp)
        cp.start()
    done = []
    slot = 0
    for g, (_, base, chunk, with_w, with_n) in enumerate(groups):
        for copy in waiting[g]:
            copy.wait()
        if g + 2 < len(groups):
            waiting[g + 2] = feed(g + 2)
        if with_n:
            if not normed_waited:
                cn.wait()
                normed_waited = True
            go[slot] = lax.dot_general(
                xs[g], nv[...], (((0,), (0,)), ((), ())), preferred_element_type=F32
            )
            for k in range(4):
                place = ids[16 + base + k]
                piece = go.at[slot, pl.ds(k * FEAT, FEAT), :]
                sem = so.at[4 * slot + k]
                row = pl.multiple_of(place % SZ * FEAT, FEAT)

                @pl.when(place < SZ)
                def _():
                    pltpu.make_async_copy(piece, mine.at[pl.ds(row, FEAT), :], sem).start()

                @pl.when(place >= SZ)
                def _():
                    pltpu.make_async_copy(piece, other.at[pl.ds(row, FEAT), :], sem).start()

                done.append(pltpu.make_async_copy(piece, mine.at[pl.ds(0, FEAT), :], sem))
            slot += 1
        if with_w:
            if g == 0 and has_acc:
                ca.wait()
            for t in range(tiles):
                rows = pl.ds(t * tile, tile)
                part = jnp.dot(xs[g, rows, :], ws[g], preferred_element_type=F32)
                if g == 0 and not has_acc:
                    acc[rows, :] = part
                else:
                    acc[rows, :] += part
                if g == len(groups) - 1:
                    out = pltpu.make_async_copy(acc.at[rows, :], gn.at[rows, :], sg.at[t])
                    out.start()
                    done.append(out)
    if last:
        cp.wait()
        gain = jnp.zeros((1, acc.shape[1]), F32)
        for t in range(tok // 128):
            rows = pl.ds(t * 128, 128)
            q = acc[rows, :] * pv[rows, :]
            gain += jnp.sum(q, axis=0, keepdims=True)
            q = q * weight[...]
            folded = q[:, 0:128] + q[:, 128:256] + q[:, 256:384] + q[:, 384:512]
            stat[:, pl.ds(t * 128, 128)] = jnp.sum(folded.T, axis=0, keepdims=True)
        gain_ref[...] = jnp.broadcast_to(gain, gain_ref.shape)
    for copy in done:
        copy.wait()


def block_kernel(name, ids, stacks, groups, w=None, normed=None, acc=None, ends=None):
    tok, ch = 1536, 512
    inner, outer = w is not None, normed is not None
    count = len(groups)
    outers = sum(g[4] for g in groups)
    has_acc, last = acc is not None, ends is not None
    anyspace = pl.BlockSpec(memory_space=pl.ANY)
    whole = pl.BlockSpec(memory_space=pltpu.VMEM)
    in_specs = [pl.BlockSpec(memory_space=pltpu.SMEM)] + [anyspace] * len(stacks)
    args = [ids, *stacks]
    dma = lambda n: pltpu.SemaphoreType.DMA((n,))
    scratch = [pltpu.VMEM((count, tok, 4 * FEAT), BF), dma(4 * count)]
    out_shape = []
    if inner:
        args.append(w)
        in_specs.append(anyspace)
        scratch += [
            pltpu.VMEM((count, 4 * FEAT, ch), BF), pltpu.VMEM((tok, ch), F32), dma(4 * count), dma(tok // 512),
        ]
        out_shape.append(jax.ShapeDtypeStruct((tok, ch), F32))
    if outer:
        args.append(normed)
        in_specs.append(anyspace)
        scratch += [
            pltpu.VMEM((tok, ch), BF), pltpu.VMEM((outers, 4 * FEAT, ch), F32),
            pltpu.SemaphoreType.DMA(()), dma(4 * outers),
        ]
        out_shape += [jax.ShapeDtypeStruct((SZ * FEAT, ch), F32)] * 2
    out_specs = [anyspace] * len(out_shape)
    if has_acc:
        in_specs.append(anyspace)
        args.append(acc)
        scratch.append(pltpu.SemaphoreType.DMA(()))
    if last:
        args += list(ends)
        in_specs += [whole, anyspace]
        out_shape += [jax.ShapeDtypeStruct((1, tok), F32), jax.ShapeDtypeStruct((8, ch), F32)]
        out_specs += [whole, whole]
        scratch += [pltpu.VMEM((tok, ch), F32), pltpu.SemaphoreType.DMA(())]
    work = 8_000_000_000 * sum(g[3] + g[4] for g in groups)
    return pl.pallas_call(
        lambda *refs: block_body(groups, len(stacks), has_acc, last, *refs),
        out_shape=tuple(out_shape),
        in_specs=in_specs,
        out_specs=tuple(out_specs),
        scratch_shapes=scratch,
        compiler_params=pltpu.CompilerParams(vmem_limit_bytes=48 * 1024 * 1024),
        cost_estimate=pl.CostEstimate(flops=work, bytes_accessed=24_000_000 * count, transcendentals=0),
        name=name,
    )(*args)


def mix_body(mine1, came1, got1, mine2, came2, got2, own, *outs):
    for c, (mine, came, got) in enumerate(((mine1, came1, got1), (mine2, came2, got2))):
        for m, out in ((0, own), (2, outs[0]), (1, outs[1]), (3, outs[2])):
            rows = slice(m * FEAT, m * FEAT + FEAT)
            value = mine[rows, :] + came[rows, :] + got[rows, :].astype(F32)
            out[c * FEAT : (c + 1) * FEAT, :] = value.astype(out.dtype)


def mix(mine1, came1, got1, mine2, came2, got2):
    ch = mine1.shape[1]
    part = pl.BlockSpec((4 * FEAT, ch), lambda i: (0, 0))
    whole = pl.BlockSpec((2 * FEAT, ch), lambda i: (0, 0))
    return pl.pallas_call(
        mix_body,
        grid=(1,),
        out_shape=(jax.ShapeDtypeStruct((2 * FEAT, ch), F32),) + (jax.ShapeDtypeStruct((2 * FEAT, ch), BF),) * 3,
        in_specs=[part] * 6,
        out_specs=(whole,) * 4,
        cost_estimate=pl.CostEstimate(flops=4_000_000, bytes_accessed=8_000_000, transcendentals=0),
        name="mix",
    )(mine1, came1, got1, mine2, came2, got2)


def parts_of(value, axis):
    spread = jnp.broadcast_to(value.reshape(1, -1), (16, value.size))
    return lax.all_to_all(spread, axis, 0, 0, tiled=True)


def total(value, axis):
    return jnp.sum(parts_of(value, axis), axis=0)


def last_body(hidden, gate, grad, normalized, weight, inverse, products, grad_hidden, grad_gate):
    for t in range(hidden.shape[0] // 128):
        part = slice(t * 128, t * 128 + 128)
        row = jnp.sum(products[:, :, part], axis=0) / DI
        mean = jnp.broadcast_to(row, (128, 128)).T
        scale = jnp.broadcast_to(inverse[:, part], (128, 128)).T
        for k in range(hidden.shape[1] // 128):
            lanes = slice(k * 128, k * 128 + 128)
            g = gate[part, lanes].astype(F32)
            sigmoid = 0.5 + 0.5 * jnp.tanh(0.5 * g)
            d = scale * (grad[part, lanes] * weight[:, lanes] - normalized[part, lanes] * mean)
            grad_hidden[part, lanes] = (d * (g * sigmoid)).astype(BF)
            slope = sigmoid * (1.0 + g * (1.0 - sigmoid))
            grad_gate[part, lanes] = (d * hidden[part, lanes].astype(F32) * slope).astype(BF)


def last(hidden, gate, grad, normalized, weight, inverse, products):
    tok, ch = hidden.shape
    tile = 512
    wide = pl.BlockSpec((tile, ch), lambda i: (i, 0))
    return pl.pallas_call(
        last_body,
        grid=(tok // tile,),
        out_shape=(jax.ShapeDtypeStruct((tok, ch), BF),) * 2,
        in_specs=[
            wide, wide, wide, wide,
            pl.BlockSpec((1, ch), lambda i: (0, 0)),
            pl.BlockSpec((1, tile), lambda i: (0, i)),
            pl.BlockSpec((16, 1, tile), lambda i: (0, 0, i)),
        ],
        out_specs=(wide, wide),
        cost_estimate=pl.CostEstimate(flops=1_000, bytes_accessed=1_000, transcendentals=0),
        name="last",
    )(hidden, gate, grad, normalized, weight, inverse, products)


def local(hidden_states, gate_values, norm_weight, out_weight, out_grad):
    seq = lax.axis_index("seq")
    place = lax.axis_index("tensor")
    core, z0 = seq % 2, seq // 2
    z1 = (z0 + jnp.where((z0 + core) % 2 == 0, 1, -1)) % SZ
    near = lambda value: [value] + [send(value, first(d)) for d in (1, -1, 2)]
    names = block_ids(core, place // 4, place % 4)
    slots = []
    for b in names:
        z = b // 2
        far = (z - z0) % 2
        side = b % 2
        partner = (z0 + jnp.where((z0 + side) % 2 == 0, 1, -1)) % SZ
        slot = far * 4 + (z - jnp.where(far == 0, z0, partner)) % SZ // 2
        slots.append(jnp.where(side == core, 0, SZ) + slot)
    ids = jnp.stack(names + slots).astype(jnp.int32)

    def gather(value):
        stack = jnp.stack([value] + [send(value, first(d)) for d in (1, -1, 2)])
        right, left = send(stack, second(1)), send(stack, second(-1))
        return stack, right, left, send(right[:2], second(1)), send(left[2:], second(-1))

    set1 = gather(out_grad[:, :FEAT])
    set2 = gather(out_grad[:, FEAT:])

    gate_wide = gate_values.astype(F32)
    sigmoid_gate = jax.nn.sigmoid(gate_wide)
    gate_silu = gate_wide * sigmoid_gate
    hidden_wide = hidden_states.astype(F32)
    gated = hidden_wide * gate_silu
    squares = total(jnp.sum(gated * gated, axis=-1), "tensor")
    inverse_rms = 1.0 / jnp.sqrt(squares / DI + 1e-05)
    normalized = gated * inverse_rms[:, None]
    normed = (normalized * norm_weight).astype(BF)
    inverse_row, normed = lax.optimization_barrier((inverse_rms[None], normed))

    def grouped(operand, chunk, with_w, with_n):
        n = operand
        parts = [[(n + j, k) for k in range(4)] for j in range(3)] + [[(n + 3, 0), (n + 3, 1), (n + 4, 0), (n + 4, 1)]]
        return [(parts[k], 4 * k, chunk, with_w, with_n) for k in range(4)]

    half = 4 * FEAT
    mine1, other1 = block_kernel("outer1", ids, set1, grouped(0, 0, 0, 1), None, normed)
    came1 = send(other1, SWAP)
    mine2, other2 = block_kernel("outer2", ids, set2, grouped(0, 1, 0, 1), None, normed)
    came2 = send(other2, SWAP)
    mate1 = (mine1[half:] + came1[half:]).astype(BF)
    mate2 = (mine2[half:] + came2[half:]).astype(BF)
    mate1, mate2, ids1 = lax.optimization_barrier((mate1, mate2, ids))
    got1, got2 = send(mate1, PARTNER), send(mate2, PARTNER)
    grad_normed, stat, gain = block_kernel(
        "inner", ids1, set1 + set2, grouped(0, 0, 1, 0) + grouped(5, 1, 1, 0), out_weight, None, None,
        (norm_weight[None], normalized),
    )
    got1, got2, stat = lax.optimization_barrier((got1, got2, stat))
    own, *outs = mix(mine1, came1, got1, mine2, came2, got2)
    rows = own
    for block, d in zip((outs[1], outs[2], outs[0]), (2, -2, 4)):
        rows = rows + send(block, along_z(d)).astype(F32)
    wide_stat = jnp.broadcast_to(stat[None], (16,) + stat.shape)
    products = lax.all_to_all(wide_stat, "tensor", 0, 0, tiled=True)
    grad_hidden, grad_gate = last(
        hidden_states, gate_values, grad_normed, normalized, norm_weight[None], inverse_row, products
    )
    gain, _ = lax.optimization_barrier((gain[0], products))
    grad_norm_weight = total(gain, "seq")
    return grad_hidden, grad_gate, rows, grad_norm_weight


def solution(mesh):
    return jax.shard_map(
        local,
        mesh=mesh,
        in_specs=(
            P("seq", "tensor"),
            P("seq", "tensor"),
            P("tensor"),
            P(None, "tensor"),
            P("seq", "tensor"),
        ),
        out_specs=(P("seq", "tensor"), P("seq", "tensor"), P("seq", "tensor"), P("tensor")),
        check_vma=False,
    )
```
